128 devices in a mesh: batch: 4 (over x), seq: 32 (over y, z, core).
Axes of the slice: x: 4, y: 4, z: 4, core: 2. Of those that a mesh axis runs over, the one named last changes fastest.
Arguments:
- tokens: bfloat16 [65536, 512], P(('batch', 'seq')), parts along dimension 0, may hold values from -50 to 50
- w_query: bfloat16 [512, 512], replicated, may hold values from -0.25 to 0.25
- w_key: bfloat16 [512, 512], replicated, may hold values from -0.25 to 0.25
- w_value: bfloat16 [512, 512], replicated, may hold values from -0.25 to 0.25
- w_output: bfloat16 [512, 512], replicated, may hold values from -0.25 to 0.25
Outputs:
- mixed: bfloat16 [65536, 512], P(('batch', 'seq')), parts along dimension 0
The draws below stay inside these ranges and needn't reach their ends.
There are 4 independent parts, one for each index of `batch`. The reference program is written for one: setup_inputs(seed, part) draws one part's arguments, and reference() takes and returns one part's arrays. A program takes and returns all parts, laid end to end along the dimension named above; an argument that names none is the same for every part. Nothing has to cross between parts.
All inputs are finite; a program needn't handle non-finite values.
Results may differ from the reference program's by a relative error of at most 0.0059.
The reference program's roundings to bfloat16 on the way (of `query`, `key_rows`, `value_rows` and `attention`) count: a program that leaves them out, or rounds other values in their place, can miss the bound.
Values sent between devices are 32-bit elements; how exact they have to be, the bound alone decides.
No kernel may reach another device: no remote copies, remote signals or barrier semaphores. Data moves between devices by JAX's collectives and lax.ppermute only.
A program may use at most 192 MiB of HBM per device.

```python
import math
import jax
import jax.numpy as jnp
from jax import lax

D = 512
HEADS = 8
HEAD_DIM = 64
BLK = 128
SEQ = 16384
NLEV = 7


def draw_tokens(key, part):
    key = jax.random.fold_in(key, 11)
    first = jax.random.fold_in(key, 0)
    base = jax.random.truncated_normal(first, -5.0, 5.0, (SEQ, D), jnp.float32)
    return base.astype(jnp.bfloat16)


def centred(rng, extent, deviation, reach, held_as=jnp.bfloat16):
    result = deviation * jax.random.normal(rng, extent, jnp.float32)
    return jnp.clip(result, min=-reach, max=reach).astype(held_as)


def setup_inputs(seed: int = 0, part: int = 0) -> dict:
    splits = jax.random.split(jax.random.key(seed), 6)
    part_splits = jax.random.split(jax.random.fold_in(splits[5], part), 6)
    tokens = draw_tokens(jax.random.fold_in(jax.random.fold_in(splits[5], part), 71), part)
    w_query = centred(splits[1], (D, D), D ** -0.5, 0.25)
    w_key = centred(splits[2], (D, D), D ** -0.5, 0.25)
    w_value = centred(splits[3], (D, D), D ** -0.5, 0.25)
    w_output = centred(splits[4], (D, D), D ** -0.5, 0.25)
    return dict(tokens=tokens, w_query=w_query, w_key=w_key, w_value=w_value, w_output=w_output)


def attend_level(query_blocks, key_blocks, value_blocks, log_weight, temper):
    scores = jnp.einsum('nshd,nbhd->nhsb', query_blocks.astype(jnp.float32), key_blocks.astype(jnp.float32)) * temper + log_weight
    row_max = lax.optimization_barrier(jnp.max(scores, axis=3))
    weights = jnp.exp(scores - row_max[..., None])
    denom = lax.optimization_barrier(jnp.sum(weights, axis=3))
    rounded = lax.optimization_barrier(weights.astype(jnp.bfloat16)).astype(jnp.float32)
    accum = jnp.einsum('nhsb,nbhd->nshd', rounded, value_blocks.astype(jnp.float32))
    heads = query_blocks.shape[2]
    return (jnp.transpose(row_max, (0, 2, 1)).reshape(-1, heads), jnp.transpose(denom, (0, 2, 1)).reshape(-1, heads), accum.reshape(-1, heads, query_blocks.shape[3]))

def combine_state(state, fresh):
    old_max, old_den, old_acc = state
    new_max, new_den, new_acc = fresh
    top = jnp.maximum(old_max, new_max)
    first = jnp.exp(old_max - top)
    second = jnp.exp(new_max - top)
    return (top, old_den * first + new_den * second, old_acc * first[..., None] + new_acc * second[..., None])

def coarse_rows(fine, level):
    count = fine.shape[0]
    return lax.optimization_barrier(jnp.mean(fine.reshape(count >> level, 1 << level, fine.shape[1]), axis=1))

def sibling_blocks(coarse, count):
    shaped = coarse.reshape(count // 2, 2, BLK, HEADS, HEAD_DIM)
    return shaped[:, ::-1].reshape(count, BLK, HEADS, HEAD_DIM).astype(jnp.bfloat16)

def reference(tokens, w_query, w_key, w_value, w_output):
    temper = 1.0 / math.sqrt(HEAD_DIM)
    query = jnp.dot(tokens, w_query, preferred_element_type=jnp.float32).astype(jnp.bfloat16)
    key_rows = jnp.dot(tokens, w_key, preferred_element_type=jnp.float32).astype(jnp.bfloat16)
    value_rows = jnp.dot(tokens, w_value, preferred_element_type=jnp.float32).astype(jnp.bfloat16)
    shape_diag = (SEQ // BLK, BLK, HEADS, HEAD_DIM)
    state = attend_level(query.reshape(shape_diag), key_rows.reshape(shape_diag), value_rows.reshape(shape_diag), 0.0, temper)
    key_wide = key_rows.astype(jnp.float32)
    value_wide = value_rows.astype(jnp.float32)
    for level in range(NLEV):
        span = BLK << level
        count = SEQ // span
        sib_key = sibling_blocks(coarse_rows(key_wide, level), count)
        sib_value = sibling_blocks(coarse_rows(value_wide, level), count)
        fresh = attend_level(query.reshape(count, span, HEADS, HEAD_DIM), sib_key, sib_value, level * math.log(2.0), temper)
        state = combine_state(state, fresh)
    attention = (state[2] / state[1][..., None]).astype(jnp.bfloat16).reshape(SEQ, D)
    return jnp.dot(attention, w_output, preferred_element_type=jnp.float32).astype(jnp.bfloat16)
```

```python
import functools
import math

import jax
import jax.numpy as jnp
from jax import lax
from jax.experimental import pallas as pl
from jax.experimental.pallas import tpu as pltpu
from jax.sharding import PartitionSpec as P

HEADS = 8
HEAD_DIM = 64
BLK = 128
D = HEADS * HEAD_DIM
LN2 = math.log(2.0)
F32 = jnp.float32
BF16 = jnp.bfloat16
VMEM = pl.BlockSpec(memory_space=pltpu.VMEM)
PARAMS = pltpu.CompilerParams(vmem_limit_bytes=48 * 1024 * 1024)


def call(body, outs, *args, scratch=()):
    return pl.pallas_call(
        body,
        out_shape=outs,
        in_specs=[VMEM] * len(args),
        out_specs=jax.tree.map(lambda _: VMEM, outs),
        scratch_shapes=list(scratch),
        compiler_params=PARAMS,
    )(*args)


def shape(*dims, dtype=F32):
    return jax.ShapeDtypeStruct(dims, dtype)


def pool_matrix(rows, cols, level):
    row = lax.broadcasted_iota(jnp.int32, (rows, cols), 0)
    col = lax.broadcasted_iota(jnp.int32, (rows, cols), 1)
    return jnp.where((col >> level) == row, 2.0**-level, 0.0).astype(BF16)


def project_kernel(x_ref, wk_ref, wv_ref, k_ref, v_ref, *coarse_refs):
    x = x_ref[...]
    for half, (w_ref, r_ref) in enumerate(((wk_ref, k_ref), (wv_ref, v_ref))):
        r_ref[...] = jnp.dot(x, w_ref[...], preferred_element_type=F32).astype(BF16)
    rows = x.shape[0]
    levels = [2, 3, 4, 5, 6]
    for level, ref in zip(levels, coarse_refs):
        pool = pool_matrix(rows >> level, rows, level)
        for half, r_ref in enumerate((k_ref, v_ref)):
            ref[:, half * D : (half + 1) * D] = jnp.dot(
                pool, r_ref[...], preferred_element_type=F32
            )


def term(keys, query, value_t):
    scores = jnp.dot(keys, query, preferred_element_type=F32)
    top = jnp.max(scores, axis=0, keepdims=True)
    weights = jnp.exp(scores - top)
    denom = jnp.sum(weights, axis=0, keepdims=True)
    numer = jnp.dot(value_t, weights.astype(BF16), preferred_element_type=F32)
    return top, denom, numer


def merge(parts):
    common = functools.reduce(jnp.maximum, [p[0] for p in parts])
    factors = [jnp.exp(p[0] - common) for p in parts]
    denom = sum(p[1] * f for p, f in zip(parts, factors))
    numer = sum(p[2] * f for p, f in zip(parts, factors))
    return common, denom, numer


def local_kernel(x_ref, wq_ref, k_ref, v_ref, q_ref, top_ref, den_ref, acc_ref, vt_ref, k1_ref, v1t_ref):
    rows = x_ref.shape[0]
    q = jnp.dot(x_ref[...], wq_ref[...], preferred_element_type=F32).astype(BF16)
    qt = (q.astype(F32) * 0.125).T
    row = lax.broadcasted_iota(jnp.int32, (D, rows), 0)
    even = (row & HEAD_DIM) == 0
    q_ref[0] = jnp.where(even, qt, 0.0).astype(BF16)
    q_ref[1] = jnp.where(even, 0.0, qt).astype(BF16)
    vt_ref[...] = v_ref[...].astype(F32).T.astype(BF16)
    pool = pool_matrix(rows // 2, rows, 1)
    k1_ref[...] = jnp.dot(pool, k_ref[...], preferred_element_type=F32).astype(BF16)
    v1 = jnp.dot(pool, v_ref[...], preferred_element_type=F32)
    v1t_ref[...] = v1.T.astype(BF16)
    for head in range(HEADS):
        pair = slice(head // 2 * 128, head // 2 * 128 + 128)
        own = slice(head * HEAD_DIM, (head + 1) * HEAD_DIM)
        for block in range(rows // BLK):
            cols = slice(block * BLK, (block + 1) * BLK)
            query = q_ref[head % 2, pair, cols]
            parts = []
            for other in (block, block ^ 1):
                span = slice(other * BLK, (other + 1) * BLK)
                parts.append(term(k_ref[span, pair], query, vt_ref[own, span]))
            far = 1 - block // 2
            span = slice(far * BLK, (far + 1) * BLK)
            top, denom, numer = term(k1_ref[span, pair], query, v1t_ref[own, span])
            parts.append((top + LN2, denom, numer))
            top, denom, numer = merge(parts)
            top_ref[head : head + 1, cols] = top
            den_ref[head : head + 1, cols] = denom
            acc_ref[own, cols] = numer


def gather_rows(refs, pieces):
    return [refs[i][lo : lo + n, :] for i, lo, n in pieces]


def stage(refs, plan, kc_ref, vct_ref):
    for slot, pieces in enumerate(plan):
        rows = jnp.concatenate(gather_rows(refs, pieces), axis=0)
        kc_ref[slot] = rows[:, :D].astype(BF16)
        vct_ref[slot] = rows[:, D:].T.astype(BF16)


def remote_terms(head, q_ref, kc_ref, vct_ref, levels):
    pair = slice(head // 2 * 128, head // 2 * 128 + 128)
    own = slice(head * HEAD_DIM, (head + 1) * HEAD_DIM)
    parts = []
    for slot, level in enumerate(levels):
        top, denom, numer = term(
            kc_ref[slot, :, pair], q_ref[head % 2, pair, :], vct_ref[slot, own, :]
        )
        parts.append((top + level * LN2, denom, numer))
    return parts


def middle_kernel(plan, levels, n, *refs):
    rows, (q_ref, top_in, den_in, acc_in) = refs[:n], refs[n : n + 4]
    top_ref, den_ref, acc_ref, kc_ref, vct_ref = refs[n + 4 :]
    stage(rows, plan, kc_ref, vct_ref)
    for head in range(HEADS):
        own = slice(head * HEAD_DIM, (head + 1) * HEAD_DIM)
        parts = remote_terms(head, q_ref, kc_ref, vct_ref, levels)
        parts.append((top_in[head : head + 1, :], den_in[head : head + 1, :], acc_in[own, :]))
        top, denom, numer = merge(parts)
        top_ref[head : head + 1, :] = top
        den_ref[head : head + 1, :] = denom
        acc_ref[own, :] = numer


def final_kernel(plan, levels, n, *refs):
    rows, (q_ref, top_in, den_in, acc_in, wo_ref) = refs[:n], refs[n : n + 5]
    out_ref, kc_ref, vct_ref, att_ref = refs[n + 5 :]
    stage(rows, plan, kc_ref, vct_ref)
    for head in range(HEADS):
        own = slice(head * HEAD_DIM, (head + 1) * HEAD_DIM)
        parts = remote_terms(head, q_ref, kc_ref, vct_ref, levels)
        parts.append((top_in[head : head + 1, :], den_in[head : head + 1, :], acc_in[own, :]))
        _, denom, numer = merge(parts)
        att_ref[own, :] = numer / denom
    att = att_ref[...].T.astype(BF16)
    out_ref[...] = jnp.dot(att, wo_ref[...], preferred_element_type=F32).astype(BF16)


def shards(tokens, w_query, w_key, w_value, w_output):
    rows = tokens.shape[0]
    count = lax.axis_size("seq")

    def swap(block, apart):
        return lax.ppermute(block, "seq", [(i, i ^ apart) for i in range(count)])

    k, v, c2, c3, c4, c5, c6 = call(
        project_kernel,
        [shape(rows, D, dtype=BF16)] * 2 + [shape(rows >> l, 2 * D) for l in range(2, 7)],
        tokens,
        w_key,
        w_value,
    )
    y1, y2, y3 = swap(c5, 8), swap(c6, 16), swap(c6, 24)
    s2 = swap(c2, 1)
    z1, z2, z3 = swap(c3, 2), swap(c4, 4), swap(c4, 6)
    g = jnp.concatenate([y1, y2, y3], axis=0)
    g1, g2, g3 = swap(g, 2), swap(g, 4), swap(g, 6)
    near = swap(jnp.concatenate([z1, z2, z3], axis=0), 1)
    far = swap(jnp.concatenate([g, g1, g2, g3], axis=0), 1)

    state = [shape(HEADS, rows), shape(HEADS, rows), shape(D, rows)]
    q, top, den, acc = call(
        local_kernel,
        [shape(2, D, rows, dtype=BF16)] + state,
        tokens,
        w_query,
        k,
        v,
        scratch=[
            pltpu.VMEM((D, rows), BF16),
            pltpu.VMEM((rows // 2, D), BF16),
            pltpu.VMEM((D, rows // 2), BF16),
        ],
    )

    def staged(slots):
        return [pltpu.VMEM((slots, BLK, D), BF16), pltpu.VMEM((slots, D, BLK), BF16)]

    arrays = [s2, z1, z2, z3, near]
    plan = [[(0, 0, 128)], [(1, 0, 64), (4, 0, 64)], [(2, 0, 32), (3, 0, 32), (4, 64, 64)]]
    top, den, acc = call(
        functools.partial(middle_kernel, plan, (2, 3, 4), len(arrays)),
        state,
        *arrays,
        q,
        top,
        den,
        acc,
        scratch=staged(3),
    )
    arrays = [g, g1, g2, g3, far]
    plan = [
        [(i, 0, 16) for i in range(4)] + [(4, 32 * i, 16) for i in range(4)],
        [(i, 16, 16) for i in range(4)] + [(4, 32 * i + 16, 16) for i in range(4)],
    ]
    return call(
        functools.partial(final_kernel, plan, (5, 6), len(arrays)),
        shape(rows, D, dtype=BF16),
        *arrays,
        q,
        top,
        den,
        acc,
        w_output,
        scratch=staged(2) + [pltpu.VMEM((D, rows), F32)],
    )


def solution(mesh):
    return jax.shard_map(
        shards,
        mesh=mesh,
        in_specs=(P(("batch", "seq"), None), P(), P(), P(), P()),
        out_specs=P(("batch", "seq"), None),
        check_vma=False,
    )
```

```python
import functools
import math

import jax
import jax.numpy as jnp
from jax import lax
from jax.experimental import pallas as pl
from jax.experimental.pallas import tpu as pltpu
from jax.sharding import PartitionSpec as P

HEADS = 8
HEAD_DIM = 64
BLK = 128
D = HEADS * HEAD_DIM
LN2 = math.log(2.0)
F32 = jnp.float32
BF16 = jnp.bfloat16
VMEM = pl.BlockSpec(memory_space=pltpu.VMEM)
PARAMS = pltpu.CompilerParams(vmem_limit_bytes=48 * 1024 * 1024)


def call(body, outs, *args, scratch=(), place=VMEM):
    return pl.pallas_call(
        body,
        out_shape=outs,
        in_specs=[place] * len(args),
        out_specs=jax.tree.map(lambda _: VMEM, outs),
        scratch_shapes=list(scratch),
        compiler_params=PARAMS,
    )(*args)


def shape(*dims, dtype=F32):
    return jax.ShapeDtypeStruct(dims, dtype)


def pool_matrix(rows, cols, level):
    row = lax.broadcasted_iota(jnp.int32, (rows, cols), 0)
    col = lax.broadcasted_iota(jnp.int32, (rows, cols), 1)
    return jnp.where((col >> level) == row, 2.0**-level, 0.0).astype(BF16)


def project_kernel(x_hbm, wk_hbm, wv_hbm, k_ref, v_ref, *refs):
    coarse_refs, (x_ref, wk_ref, wv_ref, sems) = refs[:5], refs[5:]
    copies = [
        pltpu.make_async_copy(src, dst, sems.at[i])
        for i, (src, dst) in enumerate(((x_hbm, x_ref), (wk_hbm, wk_ref), (wv_hbm, wv_ref)))
    ]
    for copy in copies:
        copy.start()
    copies[0].wait()
    for copy, w_ref, r_ref in ((copies[1], wk_ref, k_ref), (copies[2], wv_ref, v_ref)):
        copy.wait()
        r_ref[...] = jnp.dot(x_ref[...], w_ref[...], preferred_element_type=F32).astype(BF16)
    rows = x_ref.shape[0]
    levels = [2, 3, 4, 5, 6]
    for level, ref in zip(levels, coarse_refs):
        pool = pool_matrix(rows >> level, rows, level)
        for half, r_ref in enumerate((k_ref, v_ref)):
            ref[:, half * D : (half + 1) * D] = jnp.dot(
                pool, r_ref[...], preferred_element_type=F32
            )


def term(keys, query, value_t):
    scores = jnp.dot(keys, query, preferred_element_type=F32)
    top = jnp.max(scores, axis=0, keepdims=True)
    weights = jnp.exp(scores - top)
    denom = jnp.sum(weights, axis=0, keepdims=True)
    numer = jnp.dot(value_t, weights.astype(BF16), preferred_element_type=F32)
    return top, denom, numer


def merge(parts):
    common = functools.reduce(jnp.maximum, [p[0] for p in parts])
    factors = [jnp.exp(p[0] - common) for p in parts]
    denom = sum(p[1] * f for p, f in zip(parts, factors))
    numer = sum(p[2] * f for p, f in zip(parts, factors))
    return common, denom, numer


def local_kernel(x_ref, wq_ref, k_ref, v_ref, q_ref, top_ref, den_ref, acc_ref, vt_ref, k1_ref, v1t_ref):
    rows = x_ref.shape[0]
    q = jnp.dot(x_ref[...], wq_ref[...], preferred_element_type=F32).astype(BF16)
    qt = (q.astype(F32) * 0.125).T
    row = lax.broadcasted_iota(jnp.int32, (D, rows), 0)
    even = (row & HEAD_DIM) == 0
    q_ref[0] = jnp.where(even, qt, 0.0).astype(BF16)
    q_ref[1] = jnp.where(even, 0.0, qt).astype(BF16)
    vt_ref[...] = v_ref[...].astype(F32).T.astype(BF16)
    pool = pool_matrix(rows // 2, rows, 1)
    k1_ref[...] = jnp.dot(pool, k_ref[...], preferred_element_type=F32).astype(BF16)
    v1 = jnp.dot(pool, v_ref[...], preferred_element_type=F32)
    v1t_ref[...] = v1.T.astype(BF16)
    for head in range(HEADS):
        pair = slice(head // 2 * 128, head // 2 * 128 + 128)
        own = slice(head * HEAD_DIM, (head + 1) * HEAD_DIM)
        for block in range(rows // BLK):
            cols = slice(block * BLK, (block + 1) * BLK)
            query = q_ref[head % 2, pair, cols]
            parts = []
            for other in (block, block ^ 1):
                span = slice(other * BLK, (other + 1) * BLK)
                parts.append(term(k_ref[span, pair], query, vt_ref[own, span]))
            far = 1 - block // 2
            span = slice(far * BLK, (far + 1) * BLK)
            top, denom, numer = term(k1_ref[span, pair], query, v1t_ref[own, span])
            parts.append((top + LN2, denom, numer))
            top, denom, numer = merge(parts)
            top_ref[head : head + 1, cols] = top
            den_ref[head : head + 1, cols] = denom
            acc_ref[own, cols] = numer


def gather_rows(refs, pieces):
    return [refs[i][lo : lo + n, :] for i, lo, n in pieces]


def stage(refs, plan, kc_ref, vct_ref):
    for slot, pieces in enumerate(plan):
        rows = jnp.concatenate(gather_rows(refs, pieces), axis=0)
        kc_ref[slot] = rows[:, :D].astype(BF16)
        vct_ref[slot] = rows[:, D:].T.astype(BF16)


def remote_terms(head, cols, q_ref, kc_ref, vct_ref, levels):
    pair = slice(head // 2 * 128, head // 2 * 128 + 128)
    own = slice(head * HEAD_DIM, (head + 1) * HEAD_DIM)
    parts = []
    for slot, level in enumerate(levels):
        top, denom, numer = term(
            kc_ref[slot, :, pair], q_ref[head % 2, pair, cols], vct_ref[slot, own, :]
        )
        parts.append((top + level * LN2, denom, numer))
    return parts


def chunks(rows):
    for head in range(HEADS):
        for lo in range(0, rows, BLK):
            yield head, slice(head * HEAD_DIM, (head + 1) * HEAD_DIM), slice(lo, lo + BLK)


def middle_kernel(plan, levels, n, *refs):
    rows, (q_ref, top_in, den_in, acc_in) = refs[:n], refs[n : n + 4]
    top_ref, den_ref, acc_ref, kc_ref, vct_ref = refs[n + 4 :]
    stage(rows, plan, kc_ref, vct_ref)
    for head, own, cols in chunks(acc_ref.shape[1]):
        parts = remote_terms(head, cols, q_ref, kc_ref, vct_ref, levels)
        one = slice(head, head + 1)
        parts.append((top_in[one, cols], den_in[one, cols], acc_in[own, cols]))
        top_ref[one, cols], den_ref[one, cols], acc_ref[own, cols] = merge(parts)


def final_kernel(plan, levels, n, *refs):
    rows, (q_ref, top_in, den_in, acc_in, wo_ref) = refs[:n], refs[n : n + 5]
    out_ref, kc_ref, vct_ref, att_ref = refs[n + 5 :]
    stage(rows, plan, kc_ref, vct_ref)
    for head, own, cols in chunks(acc_in.shape[1]):
        parts = remote_terms(head, cols, q_ref, kc_ref, vct_ref, levels)
        one = slice(head, head + 1)
        parts.append((top_in[one, cols], den_in[one, cols], acc_in[own, cols]))
        _, denom, numer = merge(parts)
        att_ref[own, cols] = numer / denom
    att = att_ref[...].T.astype(BF16)
    out_ref[...] = jnp.dot(att, wo_ref[...], preferred_element_type=F32).astype(BF16)


def shards(tokens, w_query, w_key, w_value, w_output):
    rows = tokens.shape[0]
    count = lax.axis_size("seq")

    def swap(block, apart):
        return lax.ppermute(block, "seq", [(i, i ^ apart) for i in range(count)])

    k, v, c2, c3, c4, c5, c6 = call(
        project_kernel,
        [shape(rows, D, dtype=BF16)] * 2 + [shape(rows >> l, 2 * D) for l in range(2, 7)],
        *(pltpu.with_memory_space_constraint(a, pltpu.HBM) for a in (tokens, w_key, w_value)),
        scratch=[pltpu.VMEM((rows, D), BF16)]
        + [pltpu.VMEM((D, D), BF16)] * 2
        + [pltpu.SemaphoreType.DMA((3,))],
        place=pl.BlockSpec(memory_space=pltpu.HBM),
    )
    y1, y2, y3 = swap(c5, 8), swap(c6, 16), swap(c6, 24)
    s2 = swap(c2, 1)
    z1, z2, z3 = swap(c3, 2), swap(c4, 4), swap(c4, 6)
    state = [shape(HEADS, rows), shape(HEADS, rows), shape(D, rows)]
    q, top, den, acc = call(
        local_kernel,
        [shape(2, D, rows, dtype=BF16)] + state,
        tokens,
        w_query,
        k,
        v,
        scratch=[
            pltpu.VMEM((D, rows), BF16),
            pltpu.VMEM((rows // 2, D), BF16),
            pltpu.VMEM((D, rows // 2), BF16),
        ],
    )
    y1, y2, y3, z1, z2, z3, top = lax.optimization_barrier((y1, y2, y3, z1, z2, z3, top))
    g = jnp.concatenate([y1, y2, y3], axis=0)
    g1, g2, g3 = swap(g, 2), swap(g, 4), swap(g, 6)
    near = swap(jnp.concatenate([z1, z2, z3], axis=0), 1)
    def staged(slots):
        return [pltpu.VMEM((slots, BLK, D), BF16), pltpu.VMEM((slots, D, BLK), BF16)]

    arrays = [s2, z1, z2, z3, near]
    plan = [[(0, 0, 128)], [(1, 0, 64), (4, 0, 64)], [(2, 0, 32), (3, 0, 32), (4, 64, 64)]]
    top, den, acc = call(
        functools.partial(middle_kernel, plan, (2, 3, 4), len(arrays)),
        state,
        *arrays,
        q,
        top,
        den,
        acc,
        scratch=staged(3),
    )
    f0 = swap(g, 1)
    g1, g2, g3, top = lax.optimization_barrier((g1, g2, g3, top))
    f1, f2, f3 = [swap(part, 1) for part in (g1, g2, g3)]
    arrays = [g, g1, g2, g3, f0, f1, f2, f3]
    plan = [[(i, lo, 16) for i in range(8)] for lo in (0, 16)]
    return call(
        functools.partial(final_kernel, plan, (5, 6), len(arrays)),
        shape(rows, D, dtype=BF16),
        *arrays,
        q,
        top,
        den,
        acc,
        w_output,
        scratch=staged(2) + [pltpu.VMEM((D, rows), F32)],
    )


def solution(mesh):
    return jax.shard_map(
        shards,
        mesh=mesh,
        in_specs=(P(("batch", "seq"), None), P(), P(), P(), P()),
        out_specs=P(("batch", "seq"), None),
        check_vma=False,
    )
```

```python
import functools
import math

import jax
import jax.numpy as jnp
from jax import lax
from jax.experimental import pallas as pl
from jax.experimental.pallas import tpu as pltpu
from jax.sharding import PartitionSpec as P

HEADS = 8
HEAD_DIM = 64
BLK = 128
D = HEADS * HEAD_DIM
LN2 = math.log(2.0)
F32 = jnp.float32
BF16 = jnp.bfloat16
VMEM = pl.BlockSpec(memory_space=pltpu.VMEM)
HBM = pl.BlockSpec(memory_space=pltpu.HBM)
PARAMS = pltpu.CompilerParams(vmem_limit_bytes=48 * 1024 * 1024)


def call(body, outs, *args, scratch=(), place=VMEM, out_place=VMEM):
    return pl.pallas_call(
        body,
        out_shape=outs,
        in_specs=[place] * len(args),
        out_specs=jax.tree.map(lambda _: out_place, outs),
        scratch_shapes=list(scratch),
        compiler_params=PARAMS,
    )(*args)


def shape(*dims, dtype=F32):
    return jax.ShapeDtypeStruct(dims, dtype)


def pool_matrix(cols, levels, padded):
    row = lax.broadcasted_iota(jnp.int32, (padded, cols), 0)
    col = lax.broadcasted_iota(jnp.int32, (padded, cols), 1)
    pool = jnp.zeros((padded, cols), F32)
    first = 0
    for level in levels:
        pool = jnp.where((col >> level) == row - first, 2.0**-level, pool)
        first += cols >> level
    return pool.astype(BF16)


def project_kernel(x_hbm, wk_hbm, wv_hbm, k_ref, v_ref, *refs):
    coarse_refs, (x_ref, wk_ref, wv_ref, sems) = refs[:5], refs[5:]
    copies = [
        pltpu.make_async_copy(src, dst, sems.at[i])
        for i, (src, dst) in enumerate(((x_hbm, x_ref), (wk_hbm, wk_ref), (wv_hbm, wv_ref)))
    ]
    for copy in copies:
        copy.start()
    rows = x_ref.shape[0]
    pool = pool_matrix(rows, range(2, 7), rows // 2)
    copies[0].wait()
    for half, w_ref, r_ref in ((0, wk_ref, k_ref), (1, wv_ref, v_ref)):
        copies[1 + half].wait()
        fine = jnp.dot(x_ref[...], w_ref[...], preferred_element_type=F32).astype(BF16)
        r_ref[...] = fine
        pooled = jnp.dot(pool, fine, preferred_element_type=F32)
        first = 0
        for ref in coarse_refs:
            n = ref.shape[0]
            ref[:, half * D : (half + 1) * D] = pooled[first : first + n]
            first += n


def term(keys, query, value_t):
    scores = jnp.dot(keys, query, preferred_element_type=F32)
    top = jnp.max(scores, axis=0, keepdims=True)
    weights = jnp.exp(scores - top)
    denom = jnp.sum(weights, axis=0, keepdims=True)
    numer = jnp.dot(value_t, weights.astype(BF16), preferred_element_type=F32)
    return top, denom, numer


def merge(parts):
    common = functools.reduce(jnp.maximum, [p[0] for p in parts])
    factors = [jnp.exp(p[0] - common) for p in parts]
    denom = sum(p[1] * f for p, f in zip(parts, factors))
    numer = sum(p[2] * f for p, f in zip(parts, factors))
    return common, denom, numer


def local_kernel(x_ref, wq_ref, k_ref, v_ref, s2_ref, z1_ref, near_ref, q_ref, top_ref, den_ref, acc_ref, *scratch):
    vt_ref, k1_ref, v1t_ref, kc_ref, vct_ref = scratch
    half = BLK // 2
    plan = [[(0, 0, BLK)], [(1, 0, half), (2, 0, half)]]
    stage([s2_ref, z1_ref, near_ref], plan, kc_ref, vct_ref)
    rows = x_ref.shape[0]
    q = jnp.dot(x_ref[...], wq_ref[...], preferred_element_type=F32).astype(BF16)
    qt = (q.astype(F32) * 0.125).T
    row = lax.broadcasted_iota(jnp.int32, (D, rows), 0)
    even = (row & HEAD_DIM) == 0
    q_ref[0] = jnp.where(even, qt, 0.0).astype(BF16)
    q_ref[1] = jnp.where(even, 0.0, qt).astype(BF16)
    vt_ref[...] = v_ref[...].astype(F32).T.astype(BF16)
    pool = pool_matrix(rows, (1,), rows // 2)
    k1_ref[...] = jnp.dot(pool, k_ref[...], preferred_element_type=F32).astype(BF16)
    v1 = jnp.dot(pool, v_ref[...], preferred_element_type=F32)
    v1t_ref[...] = v1.T.astype(BF16)
    for head in range(HEADS):
        pair = slice(head // 2 * 128, head // 2 * 128 + 128)
        own = slice(head * HEAD_DIM, (head + 1) * HEAD_DIM)
        for block in range(rows // BLK):
            cols = slice(block * BLK, (block + 1) * BLK)
            query = q_ref[head % 2, pair, cols]
            parts = []
            for other in (block, block ^ 1):
                span = slice(other * BLK, (other + 1) * BLK)
                parts.append(term(k_ref[span, pair], query, vt_ref[own, span]))
            far = 1 - block // 2
            span = slice(far * BLK, (far + 1) * BLK)
            top, denom, numer = term(k1_ref[span, pair], query, v1t_ref[own, span])
            parts.append((top + LN2, denom, numer))
            parts += remote_terms(head, cols, q_ref, kc_ref, vct_ref, (2, 3))
            top, denom, numer = merge(parts)
            top_ref[head : head + 1, cols] = top
            den_ref[head : head + 1, cols] = denom
            acc_ref[own, cols] = numer


def gather_rows(refs, pieces):
    return [refs[i][lo : lo + n, :] for i, lo, n in pieces]


def stage(refs, plan, kc_ref, vct_ref):
    for slot, pieces in enumerate(plan):
        rows = jnp.concatenate(gather_rows(refs, pieces), axis=0)
        kc_ref[slot] = rows[:, :D].astype(BF16)
        vct_ref[slot] = rows[:, D:].T.astype(BF16)


def remote_terms(head, cols, q_ref, kc_ref, vct_ref, levels):
    pair = slice(head // 2 * 128, head // 2 * 128 + 128)
    own = slice(head * HEAD_DIM, (head + 1) * HEAD_DIM)
    parts = []
    for slot, level in enumerate(levels):
        top, denom, numer = term(
            kc_ref[slot, :, pair], q_ref[head % 2, pair, cols], vct_ref[slot, own, :]
        )
        parts.append((top + level * LN2, denom, numer))
    return parts


def chunks(rows):
    for head in range(HEADS):
        for lo in range(0, rows, BLK):
            yield head, slice(head * HEAD_DIM, (head + 1) * HEAD_DIM), slice(lo, lo + BLK)


def final_kernel(plan, levels, n, *refs):
    rows, (q_ref, top_in, den_in, acc_in, wo_ref) = refs[:n], refs[n : n + 5]
    out_ref, kc_ref, vct_ref, att_ref = refs[n + 5 :]
    stage(rows, plan, kc_ref, vct_ref)
    for head, own, cols in chunks(acc_in.shape[1]):
        parts = remote_terms(head, cols, q_ref, kc_ref, vct_ref, levels)
        one = slice(head, head + 1)
        parts.append((top_in[one, cols], den_in[one, cols], acc_in[own, cols]))
        _, denom, numer = merge(parts)
        att_ref[own, cols] = numer / denom
    att = att_ref[...].T.astype(BF16)
    out_ref[...] = jnp.dot(att, wo_ref[...], preferred_element_type=F32).astype(BF16)


def shards(tokens, w_query, w_key, w_value, w_output):
    rows = tokens.shape[0]
    count = lax.axis_size("seq")

    def swap(block, apart):
        return lax.ppermute(block, "seq", [(i, i ^ apart) for i in range(count)])

    k, v, c2, c3, c4, c5, c6 = call(
        project_kernel,
        [shape(rows, D, dtype=BF16)] * 2 + [shape(rows >> l, 2 * D) for l in range(2, 7)],
        *(pltpu.with_memory_space_constraint(a, pltpu.HBM) for a in (tokens, w_key, w_value)),
        scratch=[pltpu.VMEM((rows, D), BF16)]
        + [pltpu.VMEM((D, D), BF16)] * 2
        + [pltpu.SemaphoreType.DMA((3,))],
        place=HBM,
    )
    z1, z3 = swap(c3, 2), swap(c4, 6)
    y1, y2, y3 = swap(c5, 8), swap(c6, 16), swap(c6, 24)
    y1, y2, y3, z1 = lax.optimization_barrier((y1, y2, y3, z1))
    g = jnp.concatenate([y1, y2, y3], axis=0)
    near = swap(z1, 1)
    s2 = swap(c2, 1)
    f0 = swap(g, 1)
    g2 = swap(jnp.concatenate([g, c4], axis=0), 4)
    g1, g3 = swap(g, 2), swap(g, 6)
    state = [shape(HEADS, rows), shape(HEADS, rows), shape(D, rows)]
    q, top, den, acc = call(
        local_kernel,
        [shape(2, D, rows, dtype=BF16)] + state,
        tokens,
        w_query,
        k,
        v,
        s2,
        z1,
        near,
        scratch=[
            pltpu.VMEM((D, rows), BF16),
            pltpu.VMEM((rows // 2, D), BF16),
            pltpu.VMEM((D, rows // 2), BF16),
            pltpu.VMEM((2, BLK, D), BF16),
            pltpu.VMEM((2, D, BLK), BF16),
        ],
    )
    z3, g1, g2, g3, top = lax.optimization_barrier((z3, g1, g2, g3, top))
    zf = swap(z3, 1)
    def staged(slots):
        return [pltpu.VMEM((slots, BLK, D), BF16), pltpu.VMEM((slots, D, BLK), BF16)]

    f1, f2, f3 = swap(g1, 1), swap(g2, 1), swap(g3, 1)
    arrays = [g, f0, g1, f1, g2, f2, g3, f3, z3, zf]
    plan = [[(i, at, 16) for i in range(8)] for at in (0, 16)]
    plan = [[(4, 32, 32), (5, 32, 32), (8, 0, 32), (9, 0, 32)]] + plan
    return call(
        functools.partial(final_kernel, plan, (4, 5, 6), len(arrays)),
        shape(rows, D, dtype=BF16),
        *arrays,
        q,
        top,
        den,
        acc,
        w_output,
        scratch=staged(3) + [pltpu.VMEM((D, rows), F32)],
    )


def solution(mesh):
    return jax.shard_map(
        shards,
        mesh=mesh,
        in_specs=(P(("batch", "seq"), None), P(), P(), P(), P()),
        out_specs=P(("batch", "seq"), None),
        check_vma=False,
    )
```

```python
import functools
import math

import jax
import jax.numpy as jnp
from jax import lax
from jax.experimental import pallas as pl
from jax.experimental.pallas import tpu as pltpu
from jax.sharding import PartitionSpec as P

HEADS = 8
HEAD_DIM = 64
BLK = 128
D = HEADS * HEAD_DIM
LN2 = math.log(2.0)
F32 = jnp.float32
BF16 = jnp.bfloat16
VMEM = pl.BlockSpec(memory_space=pltpu.VMEM)
HBM = pl.BlockSpec(memory_space=pltpu.HBM)
PARAMS = pltpu.CompilerParams(vmem_limit_bytes=48 * 1024 * 1024)


def call(body, outs, *args, scratch=(), place=VMEM, out_place=VMEM):
    return pl.pallas_call(
        body,
        out_shape=outs,
        in_specs=[place] * len(args),
        out_specs=jax.tree.map(lambda _: out_place, outs),
        scratch_shapes=list(scratch),
        compiler_params=PARAMS,
    )(*args)


def shape(*dims, dtype=F32):
    return jax.ShapeDtypeStruct(dims, dtype)


def pool_matrix(cols, levels, padded):
    row = lax.broadcasted_iota(jnp.int32, (padded, cols), 0)
    col = lax.broadcasted_iota(jnp.int32, (padded, cols), 1)
    pool = jnp.zeros((padded, cols), F32)
    first = 0
    for level in levels:
        pool = jnp.where((col >> level) == row - first, 2.0**-level, pool)
        first += cols >> level
    return pool.astype(BF16)


def project_kernel(x_hbm, wk_hbm, wv_hbm, k_ref, v_ref, *refs):
    coarse_refs, (x_ref, wk_ref, wv_ref, sems) = refs[:5], refs[5:]
    copies = [
        pltpu.make_async_copy(src, dst, sems.at[i])
        for i, (src, dst) in enumerate(((x_hbm, x_ref), (wk_hbm, wk_ref), (wv_hbm, wv_ref)))
    ]
    for copy in copies:
        copy.start()
    rows = x_ref.shape[0]
    pool = pool_matrix(rows, range(2, 7), rows // 2)
    copies[0].wait()
    for half, w_ref, r_ref in ((0, wk_ref, k_ref), (1, wv_ref, v_ref)):
        copies[1 + half].wait()
        fine = jnp.dot(x_ref[...], w_ref[...], preferred_element_type=F32).astype(BF16)
        r_ref[...] = fine
        pooled = jnp.dot(pool, fine, preferred_element_type=F32)
        first = 0
        for ref in coarse_refs:
            n = ref.shape[0]
            ref[:, half * D : (half + 1) * D] = pooled[first : first + n]
            first += n


def term(keys, query, value_t):
    scores = jnp.dot(keys, query, preferred_element_type=F32)
    top = jnp.max(scores, axis=0, keepdims=True)
    weights = jnp.exp(scores - top)
    denom = jnp.sum(weights, axis=0, keepdims=True)
    numer = jnp.dot(value_t, weights.astype(BF16), preferred_element_type=F32)
    return top, denom, numer


def merge(parts):
    common = functools.reduce(jnp.maximum, [p[0] for p in parts])
    factors = [jnp.exp(p[0] - common) for p in parts]
    denom = sum(p[1] * f for p, f in zip(parts, factors))
    numer = sum(p[2] * f for p, f in zip(parts, factors))
    return common, denom, numer


def local_kernel(x_ref, wq_ref, k_ref, v_ref, s2_ref, z1_ref, near_ref, q_ref, top_ref, den_ref, acc_ref, *scratch):
    vt_ref, k1_ref, v1t_ref, kc_ref, vct_ref = scratch
    half = BLK // 2
    plan = [[(0, 0, BLK)], [(1, 0, half), (2, 0, half)]]
    stage([s2_ref, z1_ref, near_ref], plan, kc_ref, vct_ref)
    rows = x_ref.shape[0]
    q = jnp.dot(x_ref[...], wq_ref[...], preferred_element_type=F32).astype(BF16)
    qt = (q.astype(F32) * 0.125).T
    row = lax.broadcasted_iota(jnp.int32, (D, rows), 0)
    even = (row & HEAD_DIM) == 0
    q_ref[0] = jnp.where(even, qt, 0.0).astype(BF16)
    q_ref[1] = jnp.where(even, 0.0, qt).astype(BF16)
    vt_ref[...] = v_ref[...].astype(F32).T.astype(BF16)
    pool = pool_matrix(rows, (1,), rows // 2)
    k1_ref[...] = jnp.dot(pool, k_ref[...], preferred_element_type=F32).astype(BF16)
    v1 = jnp.dot(pool, v_ref[...], preferred_element_type=F32)
    v1t_ref[...] = v1.T.astype(BF16)
    for head in range(HEADS):
        pair = slice(head // 2 * 128, head // 2 * 128 + 128)
        own = slice(head * HEAD_DIM, (head + 1) * HEAD_DIM)
        for block in range(rows // BLK):
            cols = slice(block * BLK, (block + 1) * BLK)
            query = q_ref[head % 2, pair, cols]
            parts = []
            for other in (block, block ^ 1):
                span = slice(other * BLK, (other + 1) * BLK)
                parts.append(term(k_ref[span, pair], query, vt_ref[own, span]))
            far = 1 - block // 2
            span = slice(far * BLK, (far + 1) * BLK)
            top, denom, numer = term(k1_ref[span, pair], query, v1t_ref[own, span])
            parts.append((top + LN2, denom, numer))
            parts += remote_terms(head, cols, q_ref, kc_ref, vct_ref, (2, 3))
            top, denom, numer = merge(parts)
            top_ref[head : head + 1, cols] = top
            den_ref[head : head + 1, cols] = denom
            acc_ref[own, cols] = numer


def gather_rows(refs, pieces):
    return [refs[i][lo : lo + n, :] for i, lo, n in pieces]


def stage(refs, plan, kc_ref, vct_ref):
    for slot, pieces in enumerate(plan):
        rows = jnp.concatenate(gather_rows(refs, pieces), axis=0)
        kc_ref[slot] = rows[:, :D].astype(BF16)
        vct_ref[slot] = rows[:, D:].T.astype(BF16)


def remote_terms(head, cols, q_ref, kc_ref, vct_ref, levels):
    pair = slice(head // 2 * 128, head // 2 * 128 + 128)
    own = slice(head * HEAD_DIM, (head + 1) * HEAD_DIM)
    parts = []
    for slot, level in enumerate(levels):
        top, denom, numer = term(
            kc_ref[slot, :, pair], q_ref[head % 2, pair, cols], vct_ref[slot, own, :]
        )
        parts.append((top + level * LN2, denom, numer))
    return parts


def chunks(rows):
    for head in range(HEADS):
        for lo in range(0, rows, BLK):
            yield head, slice(head * HEAD_DIM, (head + 1) * HEAD_DIM), slice(lo, lo + BLK)


def final_kernel(plan, levels, n, *refs):
    rows, (q_ref, top_in, den_in, acc_in, wo_ref) = refs[:n], refs[n : n + 5]
    out_ref, kc_ref, vct_ref, att_ref = refs[n + 5 :]
    stage(rows, plan, kc_ref, vct_ref)
    for head, own, cols in chunks(acc_in.shape[1]):
        parts = remote_terms(head, cols, q_ref, kc_ref, vct_ref, levels)
        one = slice(head, head + 1)
        parts.append((top_in[one, cols], den_in[one, cols], acc_in[own, cols]))
        _, denom, numer = merge(parts)
        att_ref[own, cols] = numer * (1.0 / denom)
    att = att_ref[...].T.astype(BF16)
    out_ref[...] = jnp.dot(att, wo_ref[...], preferred_element_type=F32).astype(BF16)


def shards(tokens, w_query, w_key, w_value, w_output):
    rows = tokens.shape[0]
    count = lax.axis_size("seq")

    def swap(block, apart):
        return lax.ppermute(block, "seq", [(i, i ^ apart) for i in range(count)])

    k, v, c2, c3, c4, c5, c6 = call(
        project_kernel,
        [shape(rows, D, dtype=BF16)] * 2 + [shape(rows >> l, 2 * D) for l in range(2, 7)],
        *(pltpu.with_memory_space_constraint(a, pltpu.HBM) for a in (tokens, w_key, w_value)),
        scratch=[pltpu.VMEM((rows, D), BF16)]
        + [pltpu.VMEM((D, D), BF16)] * 2
        + [pltpu.SemaphoreType.DMA((3,))],
        place=HBM,
    )
    z1, z3 = swap(c3, 2), swap(c4, 6)
    y1, y2, y3 = swap(c5, 8), swap(c6, 16), swap(c6, 24)
    y1, y2, y3, z1 = lax.optimization_barrier((y1, y2, y3, z1))
    g = jnp.concatenate([y1, y2, y3], axis=0)
    near = swap(jnp.concatenate([z1, g], axis=0), 1)
    s2 = swap(c2, 1)
    g2 = swap(jnp.concatenate([g, c4], axis=0), 4)
    g1, g3 = swap(g, 2), swap(g, 6)
    state = [shape(HEADS, rows), shape(HEADS, rows), shape(D, rows)]
    q, top, den, acc = call(
        local_kernel,
        [shape(2, D, rows, dtype=BF16)] + state,
        tokens,
        w_query,
        k,
        v,
        s2,
        z1,
        near,
        scratch=[
            pltpu.VMEM((D, rows), BF16),
            pltpu.VMEM((rows // 2, D), BF16),
            pltpu.VMEM((D, rows // 2), BF16),
            pltpu.VMEM((2, BLK, D), BF16),
            pltpu.VMEM((2, D, BLK), BF16),
        ],
    )
    z3, g1, g2, g3, top = lax.optimization_barrier((z3, g1, g2, g3, top))
    zf = swap(z3, 1)
    def staged(slots):
        return [pltpu.VMEM((slots, BLK, D), BF16), pltpu.VMEM((slots, D, BLK), BF16)]

    f1, f2, f3 = swap(g1, 1), swap(g2, 1), swap(g3, 1)
    arrays = [g, near, g1, f1, g2, f2, g3, f3, z3, zf]
    plan = [
        [(i, at + (64 if i == 1 else 0), 16) for i in range(8)] for at in (0, 16)
    ]
    plan = [[(4, 32, 32), (5, 32, 32), (8, 0, 32), (9, 0, 32)]] + plan
    return call(
        functools.partial(final_kernel, plan, (4, 5, 6), len(arrays)),
        shape(rows, D, dtype=BF16),
        *arrays,
        q,
        top,
        den,
        acc,
        w_output,
        scratch=staged(3) + [pltpu.VMEM((D, rows), F32)],
    )


def solution(mesh):
    return jax.shard_map(
        shards,
        mesh=mesh,
        in_specs=(P(("batch", "seq"), None), P(), P(), P(), P()),
        out_specs=P(("batch", "seq"), None),
        check_vma=False,
    )
```

```python
import functools
import math

import jax
import jax.numpy as jnp
from jax import lax
from jax.experimental import pallas as pl
from jax.experimental.pallas import tpu as pltpu
from jax.sharding import PartitionSpec as P

HEADS = 8
HEAD_DIM = 64
BLK = 128
D = HEADS * HEAD_DIM
LN2 = math.log(2.0)
F32 = jnp.float32
BF16 = jnp.bfloat16
VMEM = pl.BlockSpec(memory_space=pltpu.VMEM)
HBM = pl.BlockSpec(memory_space=pltpu.HBM)
PARAMS = pltpu.CompilerParams(vmem_limit_bytes=48 * 1024 * 1024)


def call(body, outs, *args, scratch=(), place=VMEM, out_place=VMEM):
    return pl.pallas_call(
        body,
        out_shape=outs,
        in_specs=[place] * len(args),
        out_specs=jax.tree.map(lambda _: out_place, outs),
        scratch_shapes=list(scratch),
        compiler_params=PARAMS,
    )(*args)


def shape(*dims, dtype=F32):
    return jax.ShapeDtypeStruct(dims, dtype)


def pool_matrix(cols, levels, padded):
    row = lax.broadcasted_iota(jnp.int32, (padded, cols), 0)
    col = lax.broadcasted_iota(jnp.int32, (padded, cols), 1)
    pool = jnp.zeros((padded, cols), F32)
    first = 0
    for level in levels:
        pool = jnp.where((col >> level) == row - first, 2.0**-level, pool)
        first += cols >> level
    return pool.astype(BF16)


def project_kernel(x_hbm, wk_hbm, wv_hbm, k_ref, v_ref, *refs):
    coarse_refs, (x_ref, wk_ref, wv_ref, sems) = refs[:5], refs[5:]
    copies = [
        pltpu.make_async_copy(src, dst, sems.at[i])
        for i, (src, dst) in enumerate(((x_hbm, x_ref), (wk_hbm, wk_ref), (wv_hbm, wv_ref)))
    ]
    for copy in copies:
        copy.start()
    rows = x_ref.shape[0]
    pool = pool_matrix(rows, range(2, 7), rows // 2)
    copies[0].wait()
    for half, w_ref, r_ref in ((0, wk_ref, k_ref), (1, wv_ref, v_ref)):
        copies[1 + half].wait()
        fine = jnp.dot(x_ref[...], w_ref[...], preferred_element_type=F32).astype(BF16)
        r_ref[...] = fine
        pooled = jnp.dot(pool, fine, preferred_element_type=F32)
        first = 0
        for ref in coarse_refs:
            n = ref.shape[0]
            ref[:, half * D : (half + 1) * D] = pooled[first : first + n]
            first += n


def term(keys, query, value_t):
    scores = jnp.dot(keys, query, preferred_element_type=F32)
    top = jnp.max(scores, axis=0, keepdims=True)
    weights = jnp.exp(scores - top)
    denom = jnp.sum(weights, axis=0, keepdims=True)
    numer = jnp.dot(value_t, weights.astype(BF16), preferred_element_type=F32)
    return top, denom, numer


def merge(parts):
    common = functools.reduce(jnp.maximum, [p[0] for p in parts])
    factors = [jnp.exp(p[0] - common) for p in parts]
    denom = sum(p[1] * f for p, f in zip(parts, factors))
    numer = sum(p[2] * f for p, f in zip(parts, factors))
    return common, denom, numer


def local_kernel(x_ref, wq_ref, k_ref, v_ref, s2_ref, z1_ref, near_ref, q_ref, top_ref, den_ref, acc_ref, *scratch):
    vt_ref, k1_ref, v1t_ref, kc_ref, vct_ref = scratch
    half = BLK // 2
    plan = [[(0, 0, BLK)], [(1, 0, half), (2, 0, half)]]
    stage([s2_ref, z1_ref, near_ref], plan, kc_ref, vct_ref)
    rows = x_ref.shape[0]
    q = jnp.dot(x_ref[...], wq_ref[...], preferred_element_type=F32).astype(BF16)
    qt = (q.astype(F32) * 0.125).T
    row = lax.broadcasted_iota(jnp.int32, (D, rows), 0)
    even = (row & HEAD_DIM) == 0
    q_ref[0] = jnp.where(even, qt, 0.0).astype(BF16)
    q_ref[1] = jnp.where(even, 0.0, qt).astype(BF16)
    vt_ref[...] = v_ref[...].astype(F32).T.astype(BF16)
    pool = pool_matrix(rows, (1,), rows // 2)
    k1_ref[...] = jnp.dot(pool, k_ref[...], preferred_element_type=F32).astype(BF16)
    v1 = jnp.dot(pool, v_ref[...], preferred_element_type=F32)
    v1t_ref[...] = v1.T.astype(BF16)
    for head in range(HEADS):
        pair = slice(head // 2 * 128, head // 2 * 128 + 128)
        own = slice(head * HEAD_DIM, (head + 1) * HEAD_DIM)
        for block in range(rows // BLK):
            cols = slice(block * BLK, (block + 1) * BLK)
            query = q_ref[head % 2, pair, cols]
            parts = []
            for other in (block, block ^ 1):
                span = slice(other * BLK, (other + 1) * BLK)
                parts.append(term(k_ref[span, pair], query, vt_ref[own, span]))
            far = 1 - block // 2
            span = slice(far * BLK, (far + 1) * BLK)
            top, denom, numer = term(k1_ref[span, pair], query, v1t_ref[own, span])
            parts.append((top + LN2, denom, numer))
            parts += remote_terms(head, cols, q_ref, kc_ref, vct_ref, (2, 3))
            top, denom, numer = merge(parts)
            top_ref[head : head + 1, cols] = top
            den_ref[head : head + 1, cols] = denom
            acc_ref[own, cols] = numer


def gather_rows(refs, pieces):
    return [refs[i][lo : lo + n, :] for i, lo, n in pieces]


def stage(refs, plan, kc_ref, vct_ref):
    for slot, pieces in enumerate(plan):
        rows = jnp.concatenate(gather_rows(refs, pieces), axis=0)
        kc_ref[slot] = rows[:, :D].astype(BF16)
        vct_ref[slot] = rows[:, D:].T.astype(BF16)


def remote_terms(head, cols, q_ref, kc_ref, vct_ref, levels):
    pair = slice(head // 2 * 128, head // 2 * 128 + 128)
    own = slice(head * HEAD_DIM, (head + 1) * HEAD_DIM)
    parts = []
    for slot, level in enumerate(levels):
        top, denom, numer = term(
            kc_ref[slot, :, pair], q_ref[head % 2, pair, cols], vct_ref[slot, own, :]
        )
        parts.append((top + level * LN2, denom, numer))
    return parts


def chunks(rows):
    for head in range(HEADS):
        for lo in range(0, rows, BLK):
            yield head, slice(head * HEAD_DIM, (head + 1) * HEAD_DIM), slice(lo, lo + BLK)


def final_kernel(plan, levels, n, *refs):
    rows, (q_ref, top_in, den_in, acc_in, wo_ref) = refs[:n], refs[n : n + 5]
    out_ref, kc_ref, vct_ref, att_ref = refs[n + 5 :]
    stage(rows, plan, kc_ref, vct_ref)
    for head, own, cols in chunks(acc_in.shape[1]):
        parts = remote_terms(head, cols, q_ref, kc_ref, vct_ref, levels)
        one = slice(head, head + 1)
        parts.append((top_in[one, cols], den_in[one, cols], acc_in[own, cols]))
        _, denom, numer = merge(parts)
        att_ref[own, cols] = numer * (1.0 / denom)
    att = att_ref[...].T.astype(BF16)
    out_ref[...] = jnp.dot(att, wo_ref[...], preferred_element_type=F32).astype(BF16)


def shards(tokens, w_query, w_key, w_value, w_output):
    rows = tokens.shape[0]
    count = lax.axis_size("seq")

    def swap(block, apart):
        return lax.ppermute(block, "seq", [(i, i ^ apart) for i in range(count)])

    def beyond(block):
        return lax.ppermute(block, "seq", [(i, i ^ (24 if i & 1 else 16)) for i in range(count)])

    k, v, c2, c3, c4, c5, c6 = call(
        project_kernel,
        [shape(rows, D, dtype=BF16)] * 2 + [shape(rows >> l, 2 * D) for l in range(2, 7)],
        *(pltpu.with_memory_space_constraint(a, pltpu.HBM) for a in (tokens, w_key, w_value)),
        scratch=[pltpu.VMEM((rows, D), BF16)]
        + [pltpu.VMEM((D, D), BF16)] * 2
        + [pltpu.SemaphoreType.DMA((3,))],
        place=HBM,
    )
    z1, z3 = swap(c3, 2), swap(c4, 6)
    y1 = swap(c5, 8)
    y2 = beyond(jnp.concatenate([c6, swap(c6, 1)], axis=0))
    y1, y2, z1 = lax.optimization_barrier((y1, y2, z1))
    g = jnp.concatenate([y1, y2], axis=0)
    near = swap(jnp.concatenate([z1, g], axis=0), 1)
    s2 = swap(c2, 1)
    g2 = swap(jnp.concatenate([g, c4], axis=0), 4)
    g1, g3 = swap(g, 2), swap(g, 6)
    state = [shape(HEADS, rows), shape(HEADS, rows), shape(D, rows)]
    q, top, den, acc = call(
        local_kernel,
        [shape(2, D, rows, dtype=BF16)] + state,
        tokens,
        w_query,
        k,
        v,
        s2,
        z1,
        near,
        scratch=[
            pltpu.VMEM((D, rows), BF16),
            pltpu.VMEM((rows // 2, D), BF16),
            pltpu.VMEM((D, rows // 2), BF16),
            pltpu.VMEM((2, BLK, D), BF16),
            pltpu.VMEM((2, D, BLK), BF16),
        ],
    )
    z3, g1, g2, g3, top = lax.optimization_barrier((z3, g1, g2, g3, top))
    zf = swap(z3, 1)
    def staged(slots):
        return [pltpu.VMEM((slots, BLK, D), BF16), pltpu.VMEM((slots, D, BLK), BF16)]

    f1, f2, f3 = swap(g1, 1), swap(g2, 1), swap(g3, 1)
    arrays = [g, near, g1, f1, g2, f2, g3, f3, z3, zf]
    plan = [
        [(i, at + (64 if i == 1 else 0), 16) for i in range(8)] for at in (0, 16)
    ]
    plan = [[(4, 32, 32), (5, 32, 32), (8, 0, 32), (9, 0, 32)]] + plan
    return call(
        functools.partial(final_kernel, plan, (4, 5, 6), len(arrays)),
        shape(rows, D, dtype=BF16),
        *arrays,
        q,
        top,
        den,
        acc,
        w_output,
        scratch=staged(3) + [pltpu.VMEM((D, rows), F32)],
    )


def solution(mesh):
    return jax.shard_map(
        shards,
        mesh=mesh,
        in_specs=(P(("batch", "seq"), None), P(), P(), P(), P()),
        out_specs=P(("batch", "seq"), None),
        check_vma=False,
    )
```

```python
import functools
import math

import jax
import jax.numpy as jnp
from jax import lax
from jax.experimental import pallas as pl
from jax.experimental.pallas import tpu as pltpu
from jax.sharding import PartitionSpec as P

HEADS = 8
HEAD_DIM = 64
BLK = 128
D = HEADS * HEAD_DIM
LN2 = math.log(2.0)
F32 = jnp.float32
BF16 = jnp.bfloat16
VMEM = pl.BlockSpec(memory_space=pltpu.VMEM)
HBM = pl.BlockSpec(memory_space=pltpu.HBM)
PARAMS = pltpu.CompilerParams(vmem_limit_bytes=48 * 1024 * 1024)


def call(body, outs, *args, scratch=(), place=VMEM, out_place=VMEM):
    return pl.pallas_call(
        body,
        out_shape=outs,
        in_specs=[place] * len(args),
        out_specs=jax.tree.map(lambda _: out_place, outs),
        scratch_shapes=list(scratch),
        compiler_params=PARAMS,
    )(*args)


def shape(*dims, dtype=F32):
    return jax.ShapeDtypeStruct(dims, dtype)


def pool_matrix(cols, levels, padded):
    row = lax.broadcasted_iota(jnp.int32, (padded, cols), 0)
    col = lax.broadcasted_iota(jnp.int32, (padded, cols), 1)
    pool = jnp.zeros((padded, cols), F32)
    first = 0
    for level in levels:
        pool = jnp.where((col >> level) == row - first, 2.0**-level, pool)
        first += cols >> level
    return pool.astype(BF16)


def project_kernel(x_hbm, wk_hbm, wv_hbm, k_ref, v_ref, *refs):
    coarse_refs, (x_ref, wk_ref, wv_ref, sems) = refs[:5], refs[5:]
    copies = [
        pltpu.make_async_copy(src, dst, sems.at[i])
        for i, (src, dst) in enumerate(((x_hbm, x_ref), (wk_hbm, wk_ref), (wv_hbm, wv_ref)))
    ]
    for copy in copies:
        copy.start()
    rows = x_ref.shape[0]
    pool = pool_matrix(rows, range(2, 7), rows // 2)
    copies[0].wait()
    for half, w_ref, r_ref in ((0, wk_ref, k_ref), (1, wv_ref, v_ref)):
        copies[1 + half].wait()
        fine = jnp.dot(x_ref[...], w_ref[...], preferred_element_type=F32).astype(BF16)
        r_ref[...] = fine
        pooled = jnp.dot(pool, fine, preferred_element_type=F32)
        first = 0
        for ref in coarse_refs:
            n = ref.shape[0]
            ref[:, half * D : (half + 1) * D] = pooled[first : first + n]
            first += n


def term(keys, query, value_t):
    scores = jnp.dot(keys, query, preferred_element_type=F32)
    top = jnp.max(scores, axis=0, keepdims=True)
    weights = jnp.exp(scores - top)
    denom = jnp.sum(weights, axis=0, keepdims=True)
    numer = jnp.dot(value_t, weights.astype(BF16), preferred_element_type=F32)
    return top, denom, numer


def merge(parts):
    common = functools.reduce(jnp.maximum, [p[0] for p in parts])
    factors = [jnp.exp(p[0] - common) for p in parts]
    denom = sum(p[1] * f for p, f in zip(parts, factors))
    numer = sum(p[2] * f for p, f in zip(parts, factors))
    return common, denom, numer


def local_kernel(x_ref, wq_ref, k_ref, v_ref, s2_ref, z1_ref, near_ref, q_ref, top_ref, den_ref, acc_ref, *scratch):
    vt_ref, k1_ref, v1t_ref, kc_ref, vct_ref = scratch
    half = BLK // 2
    plan = [[(0, 0, BLK)], [(1, 0, half), (2, 0, half)]]
    stage([s2_ref, z1_ref, near_ref], plan, kc_ref, vct_ref)
    rows = x_ref.shape[0]
    q = jnp.dot(x_ref[...], wq_ref[...], preferred_element_type=F32).astype(BF16)
    qt = (q.astype(F32) * 0.125).T
    row = lax.broadcasted_iota(jnp.int32, (D, rows), 0)
    even = (row & HEAD_DIM) == 0
    q_ref[0] = jnp.where(even, qt, 0.0).astype(BF16)
    q_ref[1] = jnp.where(even, 0.0, qt).astype(BF16)
    vt_ref[...] = v_ref[...].astype(F32).T.astype(BF16)
    pool = pool_matrix(rows, (1,), rows // 2)
    k1_ref[...] = jnp.dot(pool, k_ref[...], preferred_element_type=F32).astype(BF16)
    v1 = jnp.dot(pool, v_ref[...], preferred_element_type=F32)
    v1t_ref[...] = v1.T.astype(BF16)
    for head in range(HEADS):
        pair = slice(head // 2 * 128, head // 2 * 128 + 128)
        own = slice(head * HEAD_DIM, (head + 1) * HEAD_DIM)
        for block in range(rows // BLK):
            cols = slice(block * BLK, (block + 1) * BLK)
            query = q_ref[head % 2, pair, cols]
            parts = []
            for other in (block, block ^ 1):
                span = slice(other * BLK, (other + 1) * BLK)
                parts.append(term(k_ref[span, pair], query, vt_ref[own, span]))
            far = 1 - block // 2
            span = slice(far * BLK, (far + 1) * BLK)
            top, denom, numer = term(k1_ref[span, pair], query, v1t_ref[own, span])
            parts.append((top + LN2, denom, numer))
            parts += remote_terms(head, cols, q_ref, kc_ref, vct_ref, (2, 3))
            top, denom, numer = merge(parts)
            top_ref[head : head + 1, cols] = top
            den_ref[head : head + 1, cols] = denom
            acc_ref[own, cols] = numer


def gather_rows(refs, pieces):
    return [refs[i][lo : lo + n, :] for i, lo, n in pieces]


def stage(refs, plan, kc_ref, vct_ref):
    for slot, pieces in enumerate(plan):
        rows = jnp.concatenate(gather_rows(refs, pieces), axis=0)
        kc_ref[slot] = rows[:, :D].astype(BF16)
        vct_ref[slot] = rows[:, D:].T.astype(BF16)


def remote_terms(head, cols, q_ref, kc_ref, vct_ref, levels):
    pair = slice(head // 2 * 128, head // 2 * 128 + 128)
    own = slice(head * HEAD_DIM, (head + 1) * HEAD_DIM)
    parts = []
    for slot, level in enumerate(levels):
        top, denom, numer = term(
            kc_ref[slot, :, pair], q_ref[head % 2, pair, cols], vct_ref[slot, own, :]
        )
        parts.append((top + level * LN2, denom, numer))
    return parts


def chunks(rows):
    for head in range(HEADS):
        for lo in range(0, rows, BLK):
            yield head, slice(head * HEAD_DIM, (head + 1) * HEAD_DIM), slice(lo, lo + BLK)


def final_kernel(plan, levels, n, *refs):
    rows, (q_ref, top_in, den_in, acc_in, wo_ref) = refs[:n], refs[n : n + 5]
    out_ref, kc_ref, vct_ref, att_ref = refs[n + 5 :]
    stage(rows, plan, kc_ref, vct_ref)
    for head, own, cols in chunks(acc_in.shape[1]):
        parts = remote_terms(head, cols, q_ref, kc_ref, vct_ref, levels)
        one = slice(head, head + 1)
        parts.append((top_in[one, cols], den_in[one, cols], acc_in[own, cols]))
        _, denom, numer = merge(parts)
        att_ref[own, cols] = numer * (1.0 / denom)
    att = att_ref[...].T.astype(BF16)
    out_ref[...] = jnp.dot(att, wo_ref[...], preferred_element_type=F32).astype(BF16)


def shards(tokens, w_query, w_key, w_value, w_output):
    rows = tokens.shape[0]
    count = lax.axis_size("seq")

    def swap(block, apart):
        return lax.ppermute(block, "seq", [(i, i ^ apart) for i in range(count)])

    def beyond(block):
        return lax.ppermute(block, "seq", [(i, i ^ (24 if i & 1 else 16)) for i in range(count)])

    k, v, c2, c3, c4, c5, c6 = call(
        project_kernel,
        [shape(rows, D, dtype=BF16)] * 2 + [shape(rows >> l, 2 * D) for l in range(2, 7)],
        *(pltpu.with_memory_space_constraint(a, pltpu.HBM) for a in (tokens, w_key, w_value)),
        scratch=[pltpu.VMEM((rows, D), BF16)]
        + [pltpu.VMEM((D, D), BF16)] * 2
        + [pltpu.SemaphoreType.DMA((3,))],
        place=HBM,
    )
    z1, z3 = swap(c3, 2), swap(c4, 6)
    y1 = swap(c5, 8)
    y2 = beyond(jnp.concatenate([c6, swap(c6, 1)], axis=0))
    y1, y2, z1 = lax.optimization_barrier((y1, y2, z1))
    g = jnp.concatenate([y1, y2], axis=0)
    near = swap(jnp.concatenate([z1, g], axis=0), 1)
    s2 = swap(c2, 1)
    g2 = swap(jnp.concatenate([g, c4], axis=0), 4)
    g1, g3 = swap(g, 2), swap(g, 6)
    state = [shape(HEADS, rows), shape(HEADS, rows), shape(D, rows)]
    q, top, den, acc = call(
        local_kernel,
        [shape(2, D, rows, dtype=BF16)] + state,
        tokens,
        w_query,
        k,
        v,
        s2,
        z1,
        near,
        scratch=[
            pltpu.VMEM((D, rows), BF16),
            pltpu.VMEM((rows // 2, D), BF16),
            pltpu.VMEM((D, rows // 2), BF16),
            pltpu.VMEM((2, BLK, D), BF16),
            pltpu.VMEM((2, D, BLK), BF16),
        ],
    )
    z3, g1, g2, g3, top = lax.optimization_barrier((z3, g1, g2, g3, top))
    def staged(slots):
        return [pltpu.VMEM((slots, BLK, D), BF16), pltpu.VMEM((slots, D, BLK), BF16)]

    f1, f2 = swap(jnp.concatenate([g1, g3, z3], axis=0), 1), swap(g2, 1)
    arrays = [g, near, g1, f1, g2, f2, g3, z3]
    parts = [(0, 0), (1, 64), (2, 0), (3, 0), (4, 0), (5, 0), (6, 0), (3, 32)]
    plan = [[(i, lo + at, 16) for i, lo in parts] for at in (0, 16)]
    plan = [[(4, 32, 32), (5, 32, 32), (7, 0, 32), (3, 64, 32)]] + plan
    return call(
        functools.partial(final_kernel, plan, (4, 5, 6), len(arrays)),
        shape(rows, D, dtype=BF16),
        *arrays,
        q,
        top,
        den,
        acc,
        w_output,
        scratch=staged(3) + [pltpu.VMEM((D, rows), F32)],
    )


def solution(mesh):
    return jax.shard_map(
        shards,
        mesh=mesh,
        in_specs=(P(("batch", "seq"), None), P(), P(), P(), P()),
        out_specs=P(("batch", "seq"), None),
        check_vma=False,
    )
```

```python
import functools
import math

import jax
import jax.numpy as jnp
from jax import lax
from jax.experimental import pallas as pl
from jax.experimental.pallas import tpu as pltpu
from jax.sharding import PartitionSpec as P

HEADS = 8
HEAD_DIM = 64
BLK = 128
D = HEADS * HEAD_DIM
LN2 = math.log(2.0)
F32 = jnp.float32
BF16 = jnp.bfloat16
VMEM = pl.BlockSpec(memory_space=pltpu.VMEM)
HBM = pl.BlockSpec(memory_space=pltpu.HBM)
PARAMS = pltpu.CompilerParams(vmem_limit_bytes=48 * 1024 * 1024)


def call(body, outs, *args, scratch=(), place=VMEM, out_place=VMEM):
    return pl.pallas_call(
        body,
        out_shape=outs,
        in_specs=[place] * len(args),
        out_specs=jax.tree.map(lambda _: out_place, outs),
        scratch_shapes=list(scratch),
        compiler_params=PARAMS,
    )(*args)


def shape(*dims, dtype=F32):
    return jax.ShapeDtypeStruct(dims, dtype)


def pool_matrix(cols, levels, padded):
    row = lax.broadcasted_iota(jnp.int32, (padded, cols), 0)
    col = lax.broadcasted_iota(jnp.int32, (padded, cols), 1)
    pool = jnp.zeros((padded, cols), F32)
    first = 0
    for level in levels:
        pool = jnp.where((col >> level) == row - first, 2.0**-level, pool)
        first += cols >> level
    return pool.astype(BF16)


def project_kernel(x_hbm, wk_hbm, wv_hbm, k_ref, v_ref, *refs):
    coarse_refs, (x_ref, wk_ref, wv_ref, sems) = refs[:5], refs[5:]
    copies = [
        pltpu.make_async_copy(src, dst, sems.at[i])
        for i, (src, dst) in enumerate(((x_hbm, x_ref), (wk_hbm, wk_ref), (wv_hbm, wv_ref)))
    ]
    for copy in copies:
        copy.start()
    rows = x_ref.shape[0]
    pool = pool_matrix(rows, range(2, 7), rows // 2)
    copies[0].wait()
    for half, w_ref, r_ref in ((0, wk_ref, k_ref), (1, wv_ref, v_ref)):
        copies[1 + half].wait()
        fine = jnp.dot(x_ref[...], w_ref[...], preferred_element_type=F32).astype(BF16)
        r_ref[...] = fine
        pooled = jnp.dot(pool, fine, preferred_element_type=F32)
        first = 0
        for ref in coarse_refs:
            n = ref.shape[0]
            ref[:, half * D : (half + 1) * D] = pooled[first : first + n]
            first += n


def term(keys, query, value_t):
    scores = jnp.dot(keys, query, preferred_element_type=F32)
    top = jnp.max(scores, axis=0, keepdims=True)
    weights = jnp.exp(scores - top)
    denom = jnp.sum(weights, axis=0, keepdims=True)
    numer = jnp.dot(value_t, weights.astype(BF16), preferred_element_type=F32)
    return top, denom, numer


def merge(parts):
    common = functools.reduce(jnp.maximum, [p[0] for p in parts])
    factors = [jnp.exp(p[0] - common) for p in parts]
    denom = sum(p[1] * f for p, f in zip(parts, factors))
    numer = sum(p[2] * f for p, f in zip(parts, factors))
    return common, denom, numer


def local_kernel(x_ref, wq_ref, k_ref, v_ref, s2_ref, z1_ref, near_ref, q_ref, top_ref, den_ref, acc_ref, *scratch):
    vt_ref, k1_ref, v1t_ref, kc_ref, vct_ref = scratch
    half = BLK // 2
    plan = [[(0, 0, BLK)], [(1, 0, half), (2, 0, half)]]
    stage([s2_ref, z1_ref, near_ref], plan, kc_ref, vct_ref)
    rows = x_ref.shape[0]
    q = jnp.dot(x_ref[...], wq_ref[...], preferred_element_type=F32).astype(BF16)
    qt = (q.astype(F32) * 0.125).T
    row = lax.broadcasted_iota(jnp.int32, (D, rows), 0)
    even = (row & HEAD_DIM) == 0
    q_ref[0] = jnp.where(even, qt, 0.0).astype(BF16)
    q_ref[1] = jnp.where(even, 0.0, qt).astype(BF16)
    vt_ref[...] = v_ref[...].astype(F32).T.astype(BF16)
    pool = pool_matrix(rows, (1,), rows // 2)
    k1_ref[...] = jnp.dot(pool, k_ref[...], preferred_element_type=F32).astype(BF16)
    v1 = jnp.dot(pool, v_ref[...], preferred_element_type=F32)
    v1t_ref[...] = v1.T.astype(BF16)
    for head in range(HEADS):
        pair = slice(head // 2 * 128, head // 2 * 128 + 128)
        own = slice(head * HEAD_DIM, (head + 1) * HEAD_DIM)
        for block in range(rows // BLK):
            cols = slice(block * BLK, (block + 1) * BLK)
            query = q_ref[head % 2, pair, cols]
            parts = []
            for other in (block, block ^ 1):
                span = slice(other * BLK, (other + 1) * BLK)
                parts.append(term(k_ref[span, pair], query, vt_ref[own, span]))
            far = 1 - block // 2
            span = slice(far * BLK, (far + 1) * BLK)
            top, denom, numer = term(k1_ref[span, pair], query, v1t_ref[own, span])
            parts.append((top + LN2, denom, numer))
            parts += remote_terms(head, cols, q_ref, kc_ref, vct_ref, (2, 3))
            top, denom, numer = merge(parts)
            top_ref[head : head + 1, cols] = top
            den_ref[head : head + 1, cols] = denom
            acc_ref[own, cols] = numer


def gather_rows(refs, pieces):
    return [refs[i][lo : lo + n, :] for i, lo, n in pieces]


def stage(refs, plan, kc_ref, vct_ref):
    for slot, pieces in enumerate(plan):
        rows = jnp.concatenate(gather_rows(refs, pieces), axis=0)
        kc_ref[slot] = rows[:, :D].astype(BF16)
        vct_ref[slot] = rows[:, D:].T.astype(BF16)


def remote_terms(head, cols, q_ref, kc_ref, vct_ref, levels):
    pair = slice(head // 2 * 128, head // 2 * 128 + 128)
    own = slice(head * HEAD_DIM, (head + 1) * HEAD_DIM)
    parts = []
    for slot, level in enumerate(levels):
        top, denom, numer = term(
            kc_ref[slot, :, pair], q_ref[head % 2, pair, cols], vct_ref[slot, own, :]
        )
        parts.append((top + level * LN2, denom, numer))
    return parts


def chunks(rows):
    for head in range(HEADS):
        for lo in range(0, rows, BLK):
            yield head, slice(head * HEAD_DIM, (head + 1) * HEAD_DIM), slice(lo, lo + BLK)


def final_kernel(plan, levels, n, *refs):
    rows, (q_ref, top_in, den_in, acc_in, wo_ref) = refs[:n], refs[n : n + 5]
    out_ref, kc_ref, vct_ref, att_ref = refs[n + 5 :]
    stage(rows, plan, kc_ref, vct_ref)
    for head, own, cols in chunks(acc_in.shape[1]):
        parts = remote_terms(head, cols, q_ref, kc_ref, vct_ref, levels)
        one = slice(head, head + 1)
        parts.append((top_in[one, cols], den_in[one, cols], acc_in[own, cols]))
        _, denom, numer = merge(parts)
        att_ref[own, cols] = numer * (1.0 / denom)
    att = att_ref[...].T.astype(BF16)
    out_ref[...] = jnp.dot(att, wo_ref[...], preferred_element_type=F32).astype(BF16)


def shards(tokens, w_query, w_key, w_value, w_output):
    rows = tokens.shape[0]
    count = lax.axis_size("seq")

    def swap(block, apart):
        return lax.ppermute(block, "seq", [(i, i ^ apart) for i in range(count)])

    def beyond(block):
        return lax.ppermute(block, "seq", [(i, i ^ (24 if i & 1 else 16)) for i in range(count)])

    k, v, c2, c3, c4, c5, c6 = call(
        project_kernel,
        [shape(rows, D, dtype=BF16)] * 2 + [shape(rows >> l, 2 * D) for l in range(2, 7)],
        *(pltpu.with_memory_space_constraint(a, pltpu.HBM) for a in (tokens, w_key, w_value)),
        scratch=[pltpu.VMEM((rows, D), BF16)]
        + [pltpu.VMEM((D, D), BF16)] * 2
        + [pltpu.SemaphoreType.DMA((3,))],
        place=HBM,
    )
    z1, z3 = swap(c3, 2), swap(c4, 6)
    y1 = swap(c5, 8)
    y2 = beyond(jnp.concatenate([c6, swap(c6, 1)], axis=0))
    y1, y2, z1 = lax.optimization_barrier((y1, y2, z1))
    g = jnp.concatenate([y1, y2], axis=0)
    near = swap(jnp.concatenate([z1, g], axis=0), 1)
    s2 = swap(c2, 1)
    g2 = swap(jnp.concatenate([g, c4], axis=0), 4)
    g1, g3 = swap(g, 2), swap(g, 6)
    state = [shape(HEADS, rows), shape(HEADS, rows), shape(D, rows)]
    q, top, den, acc = call(
        local_kernel,
        [shape(2, D, rows, dtype=BF16)] + state,
        tokens,
        w_query,
        k,
        v,
        s2,
        z1,
        near,
        scratch=[
            pltpu.VMEM((D, rows), BF16),
            pltpu.VMEM((rows // 2, D), BF16),
            pltpu.VMEM((D, rows // 2), BF16),
            pltpu.VMEM((2, BLK, D), BF16),
            pltpu.VMEM((2, D, BLK), BF16),
        ],
    )
    g1, g2, g3, top = lax.optimization_barrier((g1, g2, g3, top))
    zf = swap(z3, 1)
    def staged(slots):
        return [pltpu.VMEM((slots, BLK, D), BF16), pltpu.VMEM((slots, D, BLK), BF16)]

    f1, f2, f3 = swap(g1, 1), swap(g2, 1), swap(g3, 1)
    arrays = [g, near, g1, f1, g2, f2, g3, f3, z3, zf]
    plan = [
        [(i, at + (64 if i == 1 else 0), 16) for i in range(8)] for at in (0, 16)
    ]
    plan = [[(4, 32, 32), (5, 32, 32), (8, 0, 32), (9, 0, 32)]] + plan
    return call(
        functools.partial(final_kernel, plan, (4, 5, 6), len(arrays)),
        shape(rows, D, dtype=BF16),
        *arrays,
        q,
        top,
        den,
        acc,
        w_output,
        scratch=staged(3) + [pltpu.VMEM((D, rows), F32)],
    )


def solution(mesh):
    return jax.shard_map(
        shards,
        mesh=mesh,
        in_specs=(P(("batch", "seq"), None), P(), P(), P(), P()),
        out_specs=P(("batch", "seq"), None),
        check_vma=False,
    )
```
